256 devices in a mesh: sec: 32 (over x, z), tile: 8 (over y, core).
Axes of the slice: x: 4, y: 4, z: 8, core: 2. Of those that a mesh axis runs over, the one named last changes fastest.
Arguments:
- right_side: float32 [32, 8, 64, 128], P('sec', 'tile'), may hold values from -6 to 6
- anchor_diag: float32 [32, 8, 64, 128], P('sec', 'tile'), may hold values from 0.5 to 2
- intra_own: int32 [32, 8, 96], P('sec', 'tile'), may hold values from 0 to 63
- intra_far: int32 [32, 8, 96], P('sec', 'tile'), may hold values from 0 to 511
- intra_count: int32 [32, 8], P('sec', 'tile'), may hold values from 12 to 96, as said below
- inter_own: int32 [32, 8, 48], P('sec', 'tile'), may hold values from 0 to 63
- inter_prev: int32 [32, 8, 48], P('sec', 'tile'), may hold values from 0 to 63
- inter_count: int32 [32, 8], P('sec', 'tile'), may hold values from 6 to 48, as said below
- intra_stiff: bfloat16 [32, 8, 96, 128, 128], P('sec', 'tile'), as said below
- inter_stiff: bfloat16 [32, 8, 48, 128, 128], P('sec', 'tile'), as said below
Outputs:
- solution_field: float32 [32, 8, 64, 128], P('sec', 'tile')
- residual: float32 [32, 8, 64, 128], P('sec', 'tile')
The draws below stay inside these ranges and needn't reach their ends.
Inputs may be any that keep to these rules, and one draw needn't show every extreme that they name: `intra_count`: slots at or beyond the count are ignored; some tile of some section uses all 96 slots. `inter_count`: slots at or beyond the count are ignored; some tile of some section uses all 48 slots. `intra_stiff`: every block is symmetric, and each diagonal entry exceeds the sum of magnitudes of the other entries of its row. `inter_stiff`: every block is symmetric, and each diagonal entry exceeds the sum of magnitudes of the other entries of its row.
All inputs are finite; a program needn't handle non-finite values.
Results may differ from the reference program's by a relative error of at most 0.04.
Values may be sent and summed in bfloat16 or wider, within the bound.
No kernel may reach another device: no remote copies, remote signals or barrier semaphores. Data moves between devices by JAX's collectives and lax.ppermute only.
A program may use at most 64 MiB of HBM per device.

```python
import math
import jax
import jax.numpy as jnp
from jax import lax

BLK = 64
NODE = 128
MI = 96
ME = 48
ITERS = 3
SECTIONS = 32
TILES = 8


def stiff_blocks(key, lead, count):
    key_off, key_diag = jax.random.split(key)
    strength = 0.5
    noise = jax.random.uniform(key_off, lead + (count, NODE, NODE), jnp.float32, -1.0, 1.0)
    factor = jax.random.uniform(key_diag, lead + (count, NODE), jnp.float32, 1.0, 2.0)
    offdiag = 0.5 * (noise + jnp.swapaxes(noise, -1, -2)) * (0.9 * strength / (NODE - 1))
    eye = jnp.eye(NODE, dtype=jnp.float32)
    blocks = offdiag * (1.0 - eye) + eye * (strength * factor)[..., :, None]
    return blocks.astype(jnp.bfloat16)


def skewed_counts(key, slots):
    key_val, key_pick = jax.random.split(key)
    raw = jax.random.randint(key_val, (SECTIONS, TILES), 0, slots + 1)
    counts = slots // 8 + raw * raw * (slots - slots // 8) // (slots * slots)
    place = jax.random.randint(key_pick, (), 0, SECTIONS * TILES)
    counts = counts.reshape(-1).at[place].set(slots).reshape(SECTIONS, TILES)
    return counts.astype(jnp.int32)


def draw_intra_count(key, part):
    key = jax.random.fold_in(key, 21)
    return skewed_counts(key, MI)


def draw_inter_count(key, part):
    key = jax.random.fold_in(key, 22)
    return skewed_counts(key, ME)


def draw_intra_stiff(key, part):
    key = jax.random.fold_in(key, 23)
    return stiff_blocks(key, (SECTIONS, TILES), MI)


def draw_inter_stiff(key, part):
    key = jax.random.fold_in(key, 24)
    return stiff_blocks(key, (SECTIONS, TILES), ME)


def set_ends(entries, key, smallest, high):
    index_at = [jax.random.randint(jax.random.fold_in(key, axis), (), 0, length) for axis, length in enumerate(entries.shape)]
    longest = entries.shape.index(max(entries.shape))
    next_to = index_at[:longest] + [(index_at[longest] + 1) % entries.shape[longest]] + index_at[longest + 1:]
    return entries.at[tuple(index_at)].set(smallest).at[tuple(next_to)].set(high)


def level_of(stream_key, dims, cuts, low, high):
    loudness, own = 1.0, jax.random.fold_in(stream_key, 6)
    for dim, shards_of in cuts:
        draws = jnp.exp(jax.random.uniform(jax.random.fold_in(own, dim), (shards_of,), jnp.float32, low / len(cuts), high / len(cuts)))
        loudness = loudness * jnp.repeat(draws, dims[dim] // shards_of).reshape([-1 if axis == dim else 1 for axis in range(len(dims))])
    return loudness


def bell_draw(key, extent, width, bound, shards=(), held_as=jnp.bfloat16):
    values = width * jax.random.normal(key, extent, jnp.float32)
    if shards:
        values = values * level_of(key, extent, shards, -0.22, 0.18)
    return jnp.clip(values, -bound, bound).astype(held_as)


def setup_inputs(seed: int = 0) -> dict:
    seeds = jax.random.split(jax.random.key(seed), 11)
    return {
        "right_side": bell_draw(seeds[0], (SECTIONS, TILES, BLK, NODE), 1.0, 6.0, ((0, 32), (1, 8)), jnp.float32),
        "anchor_diag": jnp.clip(jnp.exp(math.log(2.0) - 1.3862944 * jax.random.uniform(seeds[1], (SECTIONS, TILES, BLK, NODE), jnp.float32) ** level_of(seeds[1], (SECTIONS, TILES, BLK, NODE), ((0, 32), (1, 8)), -0.2, 0.2)), 0.5, 2.0),
        "intra_own": set_ends(jax.random.randint(seeds[2], (SECTIONS, TILES, MI), 0, BLK), jax.random.fold_in(seeds[2], 1), 0, BLK - 1).astype(jnp.int32),
        "intra_far": set_ends(jax.random.randint(seeds[3], (SECTIONS, TILES, MI), 0, TILES * BLK), jax.random.fold_in(seeds[3], 1), 0, (TILES * BLK) - 1).astype(jnp.int32),
        "intra_count": draw_intra_count(jax.random.fold_in(seeds[10], 71), 0),
        "inter_own": set_ends(jax.random.randint(seeds[5], (SECTIONS, TILES, ME), 0, BLK), jax.random.fold_in(seeds[5], 1), 0, BLK - 1).astype(jnp.int32),
        "inter_prev": set_ends(jax.random.randint(seeds[6], (SECTIONS, TILES, ME), 0, BLK), jax.random.fold_in(seeds[6], 1), 0, BLK - 1).astype(jnp.int32),
        "inter_count": draw_inter_count(jax.random.fold_in(seeds[10], 71), 0),
        "intra_stiff": draw_intra_stiff(jax.random.fold_in(seeds[10], 71), 0),
        "inter_stiff": draw_inter_stiff(jax.random.fold_in(seeds[10], 71), 0),
    }


def couple(stiff, diff):
    def one(pair):
        return jnp.einsum("tkij,tkj->tki", pair[0].astype(jnp.float32), pair[1].astype(jnp.float32), precision=lax.Precision.HIGHEST)
    return lax.map(one, (stiff, diff))


def apply_operator(field, anchor_diag, intra_own, intra_far, intra_count, inter_own, inter_prev, inter_count, intra_stiff, inter_stiff):
    n_sec, n_tile, n_blk, n_node = field.shape
    rounded = field.astype(jnp.bfloat16)
    flat = rounded.reshape(n_sec, n_tile * n_blk, n_node)
    sec_idx = jnp.arange(n_sec)[:, None, None]
    tile_idx = jnp.arange(n_tile)[None, :, None]
    near = rounded[sec_idx, tile_idx, intra_own]
    far = flat[sec_idx, intra_far]
    diff_in = (near.astype(jnp.float32) - far.astype(jnp.float32)).astype(jnp.bfloat16)
    live_in = (jnp.arange(intra_own.shape[2])[None, None, :] < intra_count[:, :, None]).astype(jnp.float32)
    u_in = couple(intra_stiff, diff_in) * live_in[..., None]
    result = anchor_diag * field
    result = result.at[sec_idx, tile_idx, intra_own].add(u_in)
    result = result.reshape(n_sec, n_tile * n_blk, n_node).at[sec_idx, intra_far].add(-u_in).reshape(field.shape)
    before = jnp.concatenate([jnp.zeros_like(rounded[:1]), rounded[:-1]], 0)
    near_ex = rounded[sec_idx, tile_idx, inter_own]
    prev_ex = before[sec_idx, tile_idx, inter_prev]
    diff_ex = (near_ex.astype(jnp.float32) - prev_ex.astype(jnp.float32)).astype(jnp.bfloat16)
    live_ex = (jnp.arange(inter_own.shape[2])[None, None, :] < inter_count[:, :, None]).astype(jnp.float32)
    u_ex = couple(inter_stiff, diff_ex) * live_ex[..., None]
    result = result.at[sec_idx, tile_idx, inter_own].add(u_ex)
    backward = jnp.zeros_like(field).at[sec_idx, tile_idx, inter_prev].add(-u_ex)
    result = result + jnp.concatenate([backward[1:], jnp.zeros_like(backward[:1])], 0)
    return result


def reference(right_side, anchor_diag, intra_own, intra_far, intra_count, inter_own, inter_prev, inter_count, intra_stiff, inter_stiff):
    solution_field = jnp.zeros_like(right_side)
    residual, direction = right_side, right_side
    norm_now = jnp.sum(residual * residual)
    for step in range(ITERS):
        image = apply_operator(direction, anchor_diag, intra_own, intra_far, intra_count, inter_own, inter_prev, inter_count, intra_stiff, inter_stiff)
        alpha = norm_now / jnp.sum(direction * image)
        solution_field = solution_field + alpha * direction
        residual = residual - alpha * image
        norm_next = jnp.sum(residual * residual)
        direction = residual + (norm_next / norm_now) * direction
        norm_now = norm_next
    return solution_field, residual
```

```python
import functools

import jax
import jax.numpy as jnp
from jax import lax
from jax.experimental import pallas as pl
from jax.experimental.pallas import tpu as pltpu
from jax.sharding import PartitionSpec as P

ITERS = 3
F32, BF16 = jnp.float32, jnp.bfloat16
VMEM = pl.BlockSpec(memory_space=pltpu.VMEM)
CONTRACT_ROWS = (((0,), (0,)), ((), ()))
GROUP = 8


def split(x):
    high = x.astype(BF16)
    return jnp.concatenate([high, (x - high.astype(F32)).astype(BF16)], 1)


def fold(x):
    half = x.shape[1] // 2
    return x[:, :half] + x[:, half:]


def springs(hot, field, stiff_ref, u_ref):
    slots, node = u_ref.shape
    diff = fold(lax.dot_general(hot, split(field), CONTRACT_ROWS, preferred_element_type=F32))
    rows = lax.broadcasted_iota(jnp.int32, (2 * GROUP, GROUP * node), 0) % GROUP
    cols = lax.broadcasted_iota(jnp.int32, (2 * GROUP, GROUP * node), 1) // node
    own = rows == cols
    for start in range(0, slots, GROUP):
        part = diff[start : start + GROUP]
        high = part.astype(BF16).astype(F32)
        both = jnp.concatenate([high, part - high], 0)
        wide = jnp.where(own, jnp.concatenate([both] * GROUP, 1), 0.0).astype(BF16)
        block = stiff_ref[start : start + GROUP].reshape(GROUP * node, node)
        got = jnp.dot(wide, block, preferred_element_type=F32)
        u_ref[start : start + GROUP, :] = got[:GROUP] + got[GROUP:]
    u = u_ref[...]
    spread = fold(jnp.dot(hot, split(u), preferred_element_type=F32))
    return spread, jnp.sum(diff * u, axis=0, keepdims=True)


def one_hot(near, far, count, blocks):
    slots = near.shape[1]
    live = lax.broadcasted_iota(jnp.int32, (1, slots), 1) < count
    place = lax.broadcasted_iota(jnp.int32, (blocks, slots), 0)
    plus = jnp.where(live & (place == near), 1.0, 0.0)
    minus = jnp.where(live & (place == far), 1.0, 0.0)
    return (plus - minus).astype(BF16)


def intra_kernel(tile, *refs):
    own_ref, far_ref, count_ref, stiff_ref = refs[:4]
    fields = refs[4:12]
    mine_ref, other_ref, energy_ref, u_ref = refs[12:]
    blk = fields[0].shape[0]
    me = tile[0]
    far = far_ref[0]
    far_tile, far_blk = far // blk, far % blk
    there = me ^ far_tile
    place = ((there % 2) * 4 + there // 2) * blk + far_blk
    hot = one_hot(own_ref[0], place, count_ref[0, 0], 8 * blk)
    field = jnp.concatenate([f[...] for f in fields], 0)
    spread, energy = springs(hot, field, stiff_ref.at[0, 0], u_ref)
    mine_ref[...] = spread[: 4 * blk]
    other_ref[...] = spread[4 * blk :]
    energy_ref[...] = energy


def inter_kernel(own_ref, prev_ref, count_ref, stiff_ref, mine_ref, before_ref, near_ref, back_ref, energy_ref, u_ref):
    blk = mine_ref.shape[0]
    hot = one_hot(own_ref[0], prev_ref[0] + blk, count_ref[0, 0], 2 * blk)
    field = jnp.concatenate([mine_ref[...], before_ref[...]], 0)
    spread, energy = springs(hot, field, stiff_ref.at[0, 0], u_ref)
    near_ref[...] = spread[:blk]
    back_ref[...] = spread[blk:]
    energy_ref[...] = energy


def pair_kernel(mine_ref, got_ref, *outs):
    blk = outs[0].shape[0]
    for j, out in enumerate(outs):
        out[...] = mine_ref[j * blk : (j + 1) * blk] + got_ref[j * blk : (j + 1) * blk]


def image_of(anchor_ref, v_ref, parts):
    total = anchor_ref[...] * v_ref[...]
    for part in parts:
        total = total + part[...]
    return total


def sum_kernel(anchor_ref, v_ref, *refs):
    *parts, out_ref = refs
    out_ref[...] = image_of(anchor_ref, v_ref, parts)


def lane(x, index):
    total = jnp.sum(jnp.sum(x, axis=0, keepdims=True), axis=1, keepdims=True)
    return jnp.where(lax.broadcasted_iota(jnp.int32, (1, 128), 1) == index, total, 0.0)


def moment_kernel(anchor_ref, v0, v1, v2, e1, e2, e3, f1, f2, f3, out_ref):
    row = jnp.zeros((1, 128), F32)
    for k, (v, e, f) in enumerate(((v0, e1, f1), (v1, e2, f2), (v2, e3, f3))):
        square = v[...] * v[...]
        row = row + lane(square, 2 * k)
        row = row + lane(jnp.sum(anchor_ref[...] * square, axis=0, keepdims=True) + e[...] + f[...], 2 * k + 1)
    out_ref[...] = jnp.broadcast_to(row, out_ref.shape)


def quadratic(coef, moments, shift):
    total = 0.0
    for i, a in enumerate(coef):
        for j, b in enumerate(coef):
            total = total + a * b * moments[i + j + shift]
    return total


def final_kernel(sums_ref, *refs):
    *vs, x_ref, r_ref = refs
    row = jnp.sum(sums_ref[...], axis=0, keepdims=True)
    lanes = lax.broadcasted_iota(jnp.int32, row.shape, 1)
    raw = [jnp.sum(jnp.where(lanes == j, row, 0.0), axis=1, keepdims=True) for j in range(2 * ITERS)]
    sigma = raw[1] / raw[0]
    inverse = 1.0 / sigma
    moments, scale = [], 1.0 / raw[0]
    for m in raw:
        moments.append(m * scale)
        scale = scale * inverse
    zero, one = jnp.zeros_like(sigma), jnp.ones_like(sigma)
    r, p, x = [one], [one], [zero]
    rr = one
    for step in range(ITERS):
        alpha = rr / quadratic(p, moments, 1)
        x = [a + alpha * b for a, b in zip(x + [zero] * (len(p) - len(x)), p)]
        q = [zero] + p
        r = [a - alpha * b for a, b in zip(r + [zero], q)]
        if step < ITERS - 1:
            new = quadratic(r, moments, 0)
            p = [a + (new / rr) * b for a, b in zip(r, p + [zero])]
            rr = new
    power = one
    x_sum, r_sum = 0.0, 0.0
    for k in range(ITERS + 1):
        v = vs[k][...]
        r_sum = r_sum + (r[k] * power) * v
        power = power * inverse
        if k < ITERS:
            x_sum = x_sum + (x[k] * power) * v
    x_ref[...] = x_sum
    r_ref[...] = r_sum


def call(kernel, outs, *args, scratch=(), scalars=0):
    specs = [pl.BlockSpec(memory_space=pltpu.SMEM)] * scalars + [VMEM] * (len(args) - scalars)
    return pl.pallas_call(
        kernel,
        out_shape=[jax.ShapeDtypeStruct(o, F32) for o in outs],
        in_specs=specs,
        out_specs=[VMEM] * len(outs),
        scratch_shapes=[pltpu.VMEM(s, F32) for s in scratch],
        compiler_params=pltpu.CompilerParams(vmem_limit_bytes=16 * 2**20),
    )(*args)


def swap(x, by):
    return lax.ppermute(x, "tile", [(i, i ^ by) for i in range(lax.axis_size("tile"))])


def shifted(x, by):
    peers = lax.axis_size("sec")
    return lax.ppermute(x, "sec", [(i, i + by) for i in range(peers) if 0 <= i + by < peers])


def per_device(
    right_side,
    anchor_diag,
    intra_own,
    intra_far,
    intra_count,
    inter_own,
    inter_prev,
    inter_count,
    intra_stiff,
    inter_stiff,
):
    blk, node = right_side.shape[2:]
    anchor = anchor_diag[0, 0]
    tile = lax.axis_index("tile").astype(jnp.int32).reshape(1)
    field, row = (blk, node), (1, node)
    vs, energies, energies_ex = [right_side[0, 0]], [], []
    for step in range(ITERS):
        v = vs[-1]
        before = shifted(v, 1)
        here = [v] + [swap(v, 2 * j) for j in (1, 2, 3)]
        there = [swap(h, 1) for h in here]
        near, back, energy_ex = call(
            inter_kernel, (field, field, row), inter_own, inter_prev, inter_count, inter_stiff, v, before,
            scratch=((inter_own.shape[2], node),),
        )
        incoming = shifted(back, -1)
        mine, other, energy = call(
            intra_kernel, ((4 * blk, node), (4 * blk, node), row),
            tile, intra_own, intra_far, intra_count, intra_stiff, *here, *there,
            scratch=((intra_own.shape[2], node),), scalars=1,
        )
        energies.append(energy)
        energies_ex.append(energy_ex)
        if step == ITERS - 1:
            (moments,) = call(moment_kernel, ((8, node),), anchor, *vs, *energies, *energies_ex)
            mine = jnp.concatenate([mine.reshape(4, blk, node), jnp.broadcast_to(moments, (4, 8, node))], 1).reshape(-1, node)
            other = jnp.concatenate([other.reshape(4, blk, node), jnp.broadcast_to(moments, (4, 8, node))], 1).reshape(-1, node)
            got = swap(other, 1)
            parts = call(pair_kernel, ((blk + 8, node),) * 4, mine, got)
            parts = [parts[0]] + [swap(parts[j], 2 * j) for j in (1, 2, 3)]
            sums = (parts[0][blk:] + parts[1][blk:]) + (parts[2][blk:] + parts[3][blk:])
            parts = [p[:blk] for p in parts]
        else:
            got = swap(other, 1)
            parts = call(pair_kernel, (field,) * 4, mine, got)
            parts = [parts[0]] + [swap(parts[j], 2 * j) for j in (1, 2, 3)]
        (nxt,) = call(sum_kernel, (field,), anchor, v, *parts, near, incoming)
        vs.append(nxt)
    sections = lax.axis_size("sec")
    sums = lax.all_to_all(jnp.broadcast_to(sums[:1], (sections, node)), "sec", 0, 0, tiled=True)
    x, r = call(final_kernel, (field, field), sums, *vs)
    return x[None, None], r[None, None]


def solution(mesh):
    return jax.shard_map(
        per_device,
        mesh=mesh,
        in_specs=(
            P("sec", "tile", None, None),
            P("sec", "tile", None, None),
            P("sec", "tile", None),
            P("sec", "tile", None),
            P("sec", "tile"),
            P("sec", "tile", None),
            P("sec", "tile", None),
            P("sec", "tile"),
            P("sec", "tile", None, None, None),
            P("sec", "tile", None, None, None),
        ),
        out_specs=(P("sec", "tile", None, None), P("sec", "tile", None, None)),
        check_vma=False,
    )
```

```python
import functools

import jax
import jax.numpy as jnp
from jax import lax
from jax.experimental import pallas as pl
from jax.experimental.pallas import tpu as pltpu
from jax.sharding import PartitionSpec as P

ITERS = 3
ROWS = 8
HOTFLOPS = 20000000000
OPFLOPS = 0
SCATTER = "three"
F32, BF16 = jnp.float32, jnp.bfloat16
VMEM = pl.BlockSpec(memory_space=pltpu.VMEM)
CONTRACT_ROWS = (((0,), (0,)), ((), ()))
GROUP = 8


def split(x):
    high = x.astype(BF16)
    return jnp.concatenate([high, (x - high.astype(F32)).astype(BF16)], 1)


def fold(x):
    half = x.shape[1] // 2
    return x[:, :half] + x[:, half:]


def springs(hot, field, stiff_ref, u_ref):
    slots, node = u_ref.shape
    diff = fold(lax.dot_general(hot, split(field), CONTRACT_ROWS, preferred_element_type=F32))
    rows = lax.broadcasted_iota(jnp.int32, (2 * GROUP, GROUP * node), 0) % GROUP
    cols = lax.broadcasted_iota(jnp.int32, (2 * GROUP, GROUP * node), 1) // node
    own = rows == cols
    for start in range(0, slots, GROUP):
        part = diff[start : start + GROUP]
        high = part.astype(BF16).astype(F32)
        both = jnp.concatenate([high, part - high], 0)
        wide = jnp.where(own, jnp.concatenate([both] * GROUP, 1), 0.0).astype(BF16)
        block = stiff_ref[0, 0, start : start + GROUP].reshape(GROUP * node, node)
        got = jnp.dot(wide, block, preferred_element_type=F32)
        u_ref[start : start + GROUP, :] = got[:GROUP] + got[GROUP:]
    u = u_ref[...]
    spread = fold(jnp.dot(hot, split(u), preferred_element_type=F32))
    return spread, jnp.sum(diff * u, axis=0, keepdims=True)


def one_hot(near, far, count, blocks, paired=True):
    slots = near.shape[1]
    live = lax.broadcasted_iota(jnp.int32, (1, slots), 1) < count
    place = lax.broadcasted_iota(jnp.int32, (blocks, slots), 0)
    plus = jnp.where(live & (place == near), 1.0, 0.0)
    minus = jnp.where(live & paired & (place == far), 1.0, 0.0)
    return (plus - minus).astype(BF16)


def resident(ref):
    return lambda start: ref[0, 0, start : start + GROUP]


def fetched(ref, held, sems):
    pieces = sems.shape[0]
    chunk = held.shape[0] // pieces
    copies = []
    for piece in range(pieces):
        part = pl.ds(piece * chunk, chunk)
        copies.append(pltpu.make_async_copy(ref.at[0, 0, part], held.at[part], sems.at[piece]))
        copies[-1].start()

    def group(start):
        if start % chunk == 0:
            copies[start // chunk].wait()
        return held[start : start + GROUP]

    return group


def hot_kernel(section, tile, count, count_ex, *refs):
    own, far, near, prev = [r[...] for r in refs[:4]]
    hot_in, hot_ex = refs[4:]
    blk = hot_ex.shape[0] // 2
    far = far[0]
    there = tile[0] ^ (far // blk)
    place = ((there % 2) * 4 + there // 2) * blk + far % blk
    hot_in[...] = one_hot(own[0], place, count[0], 8 * blk)
    hot_ex[...] = one_hot(near[0], prev[0] + blk, count_ex[0], 2 * blk, section[0] > 0)


def pass_kernel(v_ref, out_ref):
    out_ref[...] = v_ref[...]


def operator_kernel(step, n_fields, hot_in, hot_ex, in_ref, ex_ref, anchor_ref, row_ref, before_ref, *refs):
    fields = refs[:n_fields]
    mine_ref, other_ref, back_ref, row_out, u_in, u_ex = refs[n_fields:]
    blk = before_ref.shape[0]
    field = jnp.concatenate([f[...] for f in fields], 0)
    spread, energy = springs(hot_in[...], field, in_ref, u_in)
    v = field[:blk]
    spread_ex, energy_ex = springs(hot_ex[...], jnp.concatenate([v, before_ref[...]], 0), ex_ref, u_ex)
    back_ref[...] = spread_ex[blk:]
    image = anchor_ref[...] * v
    energy = jnp.sum(image * v, axis=0, keepdims=True) + energy + energy_ex
    square = jnp.sum(v * v, axis=0, keepdims=True)
    rows = lax.broadcasted_iota(jnp.int32, row_ref.shape, 0)
    row = row_ref[...] + jnp.where(rows == 2 * step, square, 0.0) + jnp.where(rows == 2 * step + 1, energy, 0.0)
    row_out[...] = row
    mine = spread[: 4 * blk]
    other = spread[4 * blk :]
    tall = mine_ref.shape[0] // 4
    for j in range(4):
        block = mine[j * blk : (j + 1) * blk]
        if j == 0:
            block = block + image + spread_ex[:blk]
        mine_ref[j * tall : j * tall + blk, :] = block
        other_ref[j * tall : j * tall + blk, :] = other[j * blk : (j + 1) * blk]
        if tall > blk:
            mine_ref[j * tall + blk : (j + 1) * tall, :] = row
            other_ref[j * tall + blk : (j + 1) * tall, :] = row


def pair_kernel(mine_ref, got_ref, *outs):
    tall = mine_ref.shape[0] // 4
    per = 4 // len(outs)
    for place, j in enumerate((0, 3, 1, 2)):
        block = mine_ref[j * tall : (j + 1) * tall] + got_ref[j * tall : (j + 1) * tall]
        at = (place % per) * tall
        outs[place // per][at : at + tall, :] = block


def half_kernel(a_ref, b_ref, keep_ref, send_ref):
    tall = keep_ref.shape[0]
    keep_ref[...] = a_ref[:tall] + b_ref[:tall]
    send_ref[...] = a_ref[tall:] + b_ref[tall:]


def tree(values):
    while len(values) > 1:
        values = [a + b for a, b in zip(values[::2], values[1::2])]
    return values[0]


def sum_kernel(n, *refs):
    parts, incoming, out = refs[:n], refs[n], refs[n + 1]
    out[...] = tree([p[...] for p in parts]) + incoming[...]


def row_kernel(n, *refs):
    out = refs[n]
    rows = tree([p[p.shape[0] - out.shape[1] :] for p in refs[:n]])
    out[...] = jnp.broadcast_to(rows[None], out.shape)


def quadratic(coef, moments, shift):
    total = 0.0
    for i, a in enumerate(coef):
        for j, b in enumerate(coef):
            total = total + a * b * moments[i + j + shift]
    return total


def final_kernel(n, sums_ref, *refs):
    parts, incoming = refs[:n], refs[n]
    *vs, x_ref, r_ref = refs[n + 1 :]
    blk = incoming.shape[0]
    vs = [v[...] for v in vs] + [tree([p[:blk] for p in parts]) + incoming[...]]
    rows = jnp.sum(jnp.sum(sums_ref[...], axis=0), axis=1, keepdims=True)
    raw = [rows[j : j + 1] for j in range(2 * ITERS)]
    sigma = raw[1] / raw[0]
    inverse = 1.0 / sigma
    moments, scale = [], 1.0 / raw[0]
    for m in raw:
        moments.append(m * scale)
        scale = scale * inverse
    zero, one = jnp.zeros_like(sigma), jnp.ones_like(sigma)
    r, p, x = [one], [one], [zero]
    rr = one
    for step in range(ITERS):
        alpha = rr / quadratic(p, moments, 1)
        x = [a + alpha * b for a, b in zip(x + [zero] * (len(p) - len(x)), p)]
        q = [zero] + p
        r = [a - alpha * b for a, b in zip(r + [zero], q)]
        if step < ITERS - 1:
            new = quadratic(r, moments, 0)
            p = [a + (new / rr) * b for a, b in zip(r, p + [zero])]
            rr = new
    power = one
    x_sum, r_sum = 0.0, 0.0
    for k in range(ITERS + 1):
        v = vs[k]
        r_sum = r_sum + (r[k] * power) * v
        power = power * inverse
        if k < ITERS:
            x_sum = x_sum + (x[k] * power) * v
    x_ref[...] = x_sum
    r_ref[...] = r_sum


def call(kernel, outs, *args, scratch=(), scalars=0, dtype=F32, flops=0, hbm=False, limit=16):
    specs = [pl.BlockSpec(memory_space=pltpu.SMEM)] * scalars
    specs += [pl.BlockSpec(memory_space=pltpu.HBM) if hbm else VMEM] * (len(args) - scalars)
    dtypes = dtype if isinstance(dtype, tuple) else (dtype,) * len(outs)
    return pl.pallas_call(
        kernel,
        out_shape=[jax.ShapeDtypeStruct(o, d) for o, d in zip(outs, dtypes)],
        in_specs=specs,
        out_specs=[VMEM] * len(outs),
        scratch_shapes=scratch,
        compiler_params=pltpu.CompilerParams(vmem_limit_bytes=limit * 2**20),
        cost_estimate=pl.CostEstimate(flops=flops, bytes_accessed=0, transcendentals=0) if flops else None,
    )(*args)


def swap(x, by):
    return lax.ppermute(x, "tile", [(i, i ^ by) for i in range(lax.axis_size("tile"))])


def shifted(x, by):
    peers = lax.axis_size("sec")
    return lax.ppermute(x, "sec", [(i, (i + by) % peers) for i in range(peers)])


def per_device(
    right_side,
    anchor_diag,
    intra_own,
    intra_far,
    intra_count,
    inter_own,
    inter_prev,
    inter_count,
    intra_stiff,
    inter_stiff,
):
    blk, node = right_side.shape[2:]
    anchor = anchor_diag[0, 0]
    section = lax.axis_index("sec").astype(jnp.int32).reshape(1)
    tile = lax.axis_index("tile").astype(jnp.int32).reshape(1)
    field, row = (blk, node), (ROWS, node)
    vs, moments = [right_side[0, 0]], jnp.zeros(row, F32)
    sections = lax.axis_size("sec")
    hot = call(
        hot_kernel, ((lax.axis_size("tile") * blk, intra_own.shape[2]), (2 * blk, inter_own.shape[2])),
        section, tile, intra_count.reshape(1), inter_count.reshape(1), intra_own, intra_far, inter_own, inter_prev, scalars=4, dtype=BF16,
    )
    (early,) = call(pass_kernel, (field,), vs[0], flops=HOTFLOPS)
    for step in range(ITERS):
        last = step == ITERS - 1
        tall = blk + ROWS if last else blk
        v = vs[-1]
        here = [v] + [swap(v, 2 * j) for j in (1, 2, 3)]
        if step == 0:
            v = early
        fields = here + [swap(h, 1) for h in [v] + here[1:]]
        before = shifted(v, 1)
        mine, other, back, moments = call(
            functools.partial(operator_kernel, step, len(fields)), ((4 * tall, node), (4 * tall, node), field, row),
            *hot, intra_stiff, inter_stiff, anchor, moments, before, *fields,
            scratch=[pltpu.VMEM((intra_own.shape[2], node), F32), pltpu.VMEM((inter_own.shape[2], node), F32)], flops=OPFLOPS,
        )
        incoming = shifted(back, -1)
        got = swap(other, 1)
        if SCATTER == "three":
            p0, p3, p1, p2 = call(pair_kernel, ((tall, node),) * 4, mine, got)
            parts = [p0] + [swap(p, 2 * j) for j, p in ((1, p1), (2, p2), (3, p3))]
        else:
            keep, send = call(pair_kernel, ((2 * tall, node),) * 2, mine, got)
            keep, send = call(half_kernel, ((tall, node),) * 2, keep, swap(send, 2))
            parts = [keep, swap(send, 6)]
        if not last:
            (nxt,) = call(functools.partial(sum_kernel, len(parts)), (field,), *parts, incoming)
            vs.append(nxt)
    (sums,) = call(functools.partial(row_kernel, len(parts)), ((sections, ROWS, node),), *parts)
    sums = lax.all_to_all(sums, "sec", 0, 0, tiled=True)
    x, r = call(functools.partial(final_kernel, len(parts)), (field, field), sums, *parts, incoming, *vs)
    return x[None, None], r[None, None]


def solution(mesh):
    return jax.shard_map(
        per_device,
        mesh=mesh,
        in_specs=(
            P("sec", "tile", None, None),
            P("sec", "tile", None, None),
            P("sec", "tile", None),
            P("sec", "tile", None),
            P("sec", "tile"),
            P("sec", "tile", None),
            P("sec", "tile", None),
            P("sec", "tile"),
            P("sec", "tile", None, None, None),
            P("sec", "tile", None, None, None),
        ),
        out_specs=(P("sec", "tile", None, None), P("sec", "tile", None, None)),
        check_vma=False,
    )
```

```python
import functools

import jax
import jax.numpy as jnp
from jax import lax
from jax.experimental import pallas as pl
from jax.experimental.pallas import tpu as pltpu
from jax.sharding import PartitionSpec as P

ITERS = 3
LARGE, ROUNDS = 1e37, 8
ROWS = 8
PASS_FLOPS = 20_000_000_000
F32, BF16 = jnp.float32, jnp.bfloat16
VMEM = pl.BlockSpec(memory_space=pltpu.VMEM)
CONTRACT_ROWS = (((0,), (0,)), ((), ()))
GROUP = 8


def split(x):
    high = x.astype(BF16)
    return jnp.concatenate([high, (x - high.astype(F32)).astype(BF16)], 1)


def fold(x):
    half = x.shape[1] // 2
    return x[:, :half] + x[:, half:]


def springs(hot, field, stiff_ref, scale, u_ref):
    slots, node = u_ref.shape
    diff = fold(lax.dot_general(hot, split(field), CONTRACT_ROWS, preferred_element_type=F32))
    rows = lax.broadcasted_iota(jnp.int32, (2 * GROUP, GROUP * node), 0) % GROUP
    cols = lax.broadcasted_iota(jnp.int32, (2 * GROUP, GROUP * node), 1) // node
    own = rows == cols
    for start in range(0, slots, GROUP):
        part = diff[start : start + GROUP]
        high = part.astype(BF16).astype(F32)
        both = jnp.concatenate([high, part - high], 0)
        wide = jnp.where(own, jnp.concatenate([both] * GROUP, 1), 0.0).astype(BF16)
        block = stiff_ref[0, 0, start : start + GROUP].reshape(GROUP * node, node)
        got = jnp.dot(wide, block, preferred_element_type=F32)
        u_ref[start : start + GROUP, :] = got[:GROUP] + got[GROUP:]
    u = u_ref[...] * scale
    spread = fold(jnp.dot(hot, split(u), preferred_element_type=F32))
    return spread, jnp.sum(diff * u, axis=0, keepdims=True)


def one_hot(near, far, count, blocks, paired=True):
    slots = near.shape[1]
    live = lax.broadcasted_iota(jnp.int32, (1, slots), 1) < count
    place = lax.broadcasted_iota(jnp.int32, (blocks, slots), 0)
    plus = jnp.where(live & (place == near), 1.0, 0.0)
    minus = jnp.where(live & paired & (place == far), 1.0, 0.0)
    return (plus - minus).astype(BF16)


def resident(ref):
    return lambda start: ref[0, 0, start : start + GROUP]


def fetched(ref, held, sems):
    pieces = sems.shape[0]
    chunk = held.shape[0] // pieces
    copies = []
    for piece in range(pieces):
        part = pl.ds(piece * chunk, chunk)
        copies.append(pltpu.make_async_copy(ref.at[0, 0, part], held.at[part], sems.at[piece]))
        copies[-1].start()

    def group(start):
        if start % chunk == 0:
            copies[start // chunk].wait()
        return held[start : start + GROUP]

    return group


def hot_kernel(section, tile, count, count_ex, *refs):
    own, far, near, prev = [r[...] for r in refs[:4]]
    hot_in, hot_ex = refs[5:]
    blk = hot_ex.shape[0] // 2
    far = far[0]
    there = tile[0] ^ (far // blk)
    place = ((there % 2) * 4 + there // 2) * blk + far % blk
    hot_in[...] = one_hot(own[0], place, count[0], 8 * blk)
    hot_ex[...] = one_hot(near[0], prev[0] + blk, count_ex[0], 2 * blk, section[0] > 0)


def zero_kernel(*outs):
    for out in outs:
        out[...] = jnp.zeros(out.shape, F32)


def pass_kernel(inverse, v_ref, out_ref, scale_ref):
    out_ref[...] = v_ref[...]
    scale_ref[...] = jnp.full(scale_ref.shape, inverse[0], F32)


def operator_kernel(step, n_fields, hot_in, hot_ex, scale_ref, in_ref, ex_ref, anchor_ref, row_ref, before_ref, *refs):
    fields = refs[:n_fields]
    mine_ref, other_ref, back_ref, row_out, u_in, u_ex = refs[n_fields:]
    blk = before_ref.shape[0]
    scale = scale_ref[...]
    field = jnp.concatenate([f[...] for f in fields], 0)
    spread, energy = springs(hot_in[...], field, in_ref, scale, u_in)
    v = field[:blk]
    spread_ex, energy_ex = springs(hot_ex[...], jnp.concatenate([v, before_ref[...]], 0), ex_ref, scale, u_ex)
    back_ref[...] = spread_ex[blk:]
    image = anchor_ref[...] * v * scale
    energy = jnp.sum(image * v, axis=0, keepdims=True) + energy + energy_ex
    square = jnp.sum(v * v, axis=0, keepdims=True)
    rows = lax.broadcasted_iota(jnp.int32, row_ref.shape, 0)
    row = row_ref[...] + jnp.where(rows == 2 * step, square, 0.0) + jnp.where(rows == 2 * step + 1, energy, 0.0)
    row_out[...] = row
    mine = spread[: 4 * blk]
    other = spread[4 * blk :]
    tall = mine_ref.shape[0] // 4
    for j in range(4):
        block = mine[j * blk : (j + 1) * blk]
        if j == 0:
            block = block + image + spread_ex[:blk]
        mine_ref[j * tall : j * tall + blk, :] = block
        other_ref[j * tall : j * tall + blk, :] = other[j * blk : (j + 1) * blk]
        if tall > blk:
            mine_ref[j * tall + blk : (j + 1) * tall, :] = row
            other_ref[j * tall + blk : (j + 1) * tall, :] = row


def pair_kernel(mine_ref, got_ref, *outs):
    tall = mine_ref.shape[0] // 4
    for out, j in zip(outs, (0, 3, 1, 2)):
        out[...] = mine_ref[j * tall : (j + 1) * tall] + got_ref[j * tall : (j + 1) * tall]


def tree(values):
    while len(values) > 1:
        values = [a + b for a, b in zip(values[::2], values[1::2])]
    return values[0]


def sum_kernel(n, *refs):
    parts, incoming, out = refs[:n], refs[n], refs[n + 1]
    out[...] = tree([p[...] for p in parts]) + incoming[...]


def row_kernel(n, *refs):
    out = refs[n]
    rows = tree([p[p.shape[0] - out.shape[1] :] for p in refs[:n]])
    out[...] = jnp.broadcast_to(rows[None], out.shape)


def quadratic(coef, moments, shift):
    total = 0.0
    for i, a in enumerate(coef):
        for j, b in enumerate(coef):
            total = total + a * b * moments[i + j + shift]
    return total


def final_kernel(n, sums_ref, scale_ref, *refs):
    parts, incoming = refs[:n], refs[n]
    *vs, x_ref, r_ref, again_ref, ratio_ref = refs[n + 1 :]
    blk = incoming.shape[0]
    vs = [v[...] for v in vs] + [tree([p[:blk] for p in parts]) + incoming[...]]
    rows = jnp.sum(jnp.sum(sums_ref[...], axis=0), axis=1, keepdims=True)
    raw = [rows[j : j + 1] for j in range(2 * ITERS)]
    sigma = raw[1] / raw[0]
    inverse = 1.0 / sigma
    moments, scale = [], 1.0 / raw[0]
    for m in raw:
        moments.append(m * scale)
        scale = scale * inverse
    zero, one = jnp.zeros_like(sigma), jnp.ones_like(sigma)
    r, p, x = [one], [one], [zero]
    rr = one
    for step in range(ITERS):
        alpha = rr / quadratic(p, moments, 1)
        x = [a + alpha * b for a, b in zip(x + [zero] * (len(p) - len(x)), p)]
        q = [zero] + p
        r = [a - alpha * b for a, b in zip(r + [zero], q)]
        if step < ITERS - 1:
            new = quadratic(r, moments, 0)
            p = [a + (new / rr) * b for a, b in zip(r, p + [zero])]
            rr = new
    power = one
    x_sum, r_sum = 0.0, 0.0
    for k in range(ITERS + 1):
        v = vs[k]
        r_sum = r_sum + (r[k] * power) * v
        power = power * inverse
        if k < ITERS:
            x_sum = x_sum + (x[k] * power) * v
    x_ref[...] = x_sum * scale_ref[...]
    r_ref[...] = r_sum
    fine, ratio = jnp.abs(raw[1]) < LARGE, raw[0] / raw[1]
    for before, m in zip(raw[1:], raw[2:]):
        ratio = jnp.where(m < LARGE, before / m, ratio)
        fine = fine & (m < LARGE)
    again_ref[0] = jnp.max(jnp.where(fine, 0, 1))
    ratio_ref[0] = jnp.max(ratio)


def call(kernel, outs, *args, scratch=(), scalars=0, dtype=F32, flops=0, hbm=False, limit=16, scalar_outs=0):
    specs = [pl.BlockSpec(memory_space=pltpu.SMEM)] * scalars
    specs += [pl.BlockSpec(memory_space=pltpu.HBM) if hbm else VMEM] * (len(args) - scalars)
    dtypes = dtype if isinstance(dtype, tuple) else (dtype,) * len(outs)
    return pl.pallas_call(
        kernel,
        out_shape=[jax.ShapeDtypeStruct(o, d) for o, d in zip(outs, dtypes)],
        in_specs=specs,
        out_specs=[VMEM] * (len(outs) - scalar_outs) + [pl.BlockSpec(memory_space=pltpu.SMEM)] * scalar_outs,
        scratch_shapes=scratch,
        compiler_params=pltpu.CompilerParams(vmem_limit_bytes=limit * 2**20),
        cost_estimate=pl.CostEstimate(flops=flops, bytes_accessed=0, transcendentals=0) if flops else None,
    )(*args)


def swap(x, by):
    return lax.ppermute(x, "tile", [(i, i ^ by) for i in range(lax.axis_size("tile"))])


def shifted(x, by):
    peers = lax.axis_size("sec")
    return lax.ppermute(x, "sec", [(i, (i + by) % peers) for i in range(peers)])


def one_round(
    inverse,
    right_side,
    anchor_diag,
    intra_own,
    intra_far,
    intra_count,
    inter_own,
    inter_prev,
    inter_count,
    intra_stiff,
    inter_stiff,
):
    blk, node = right_side.shape[2:]
    anchor = anchor_diag[0, 0]
    section = lax.axis_index("sec").astype(jnp.int32).reshape(1)
    tile = lax.axis_index("tile").astype(jnp.int32).reshape(1)
    field, row = (blk, node), (ROWS, node)
    vs, moments = [right_side[0, 0]], jnp.zeros(row, F32)
    sections = lax.axis_size("sec")
    vs[0], scale = call(pass_kernel, (field, (1, node)), inverse, vs[0], scalars=1, flops=PASS_FLOPS)
    hot = call(
        hot_kernel, ((lax.axis_size("tile") * blk, intra_own.shape[2]), (2 * blk, inter_own.shape[2])),
        section, tile, intra_count.reshape(1), inter_count.reshape(1), intra_own, intra_far, inter_own, inter_prev, scale,
        scalars=4, dtype=BF16,
    )
    for step in range(ITERS):
        last = step == ITERS - 1
        tall = blk + ROWS if last else blk
        v = vs[-1]
        here = [v] + [swap(v, 2 * j) for j in (1, 2, 3)]
        fields = here + [swap(h, 1) for h in here]
        before = shifted(v, 1)
        mine, other, back, moments = call(
            functools.partial(operator_kernel, step, len(fields)), ((4 * tall, node), (4 * tall, node), field, row),
            *hot, scale, intra_stiff, inter_stiff, anchor, moments, before, *fields,
            scratch=[pltpu.VMEM((intra_own.shape[2], node), F32), pltpu.VMEM((inter_own.shape[2], node), F32)],
        )
        incoming = shifted(back, -1)
        got = swap(other, 1)
        p0, p3, p1, p2 = call(pair_kernel, ((tall, node),) * 4, mine, got)
        parts = [p0] + [swap(p, 2 * j) for j, p in ((1, p1), (2, p2), (3, p3))]
        if not last:
            (nxt,) = call(functools.partial(sum_kernel, len(parts)), (field,), *parts, incoming)
            vs.append(nxt)
    (sums,) = call(functools.partial(row_kernel, len(parts)), ((sections, ROWS, node),), *parts)
    sums = lax.all_to_all(sums, "sec", 0, 0, tiled=True)
    x, r, again, ratio = call(
        functools.partial(final_kernel, len(parts)), (field, field, (1,), (1,)), sums, scale, *parts, incoming, *vs,
        dtype=(F32, F32, jnp.int32, F32), scalar_outs=2,
    )
    return again, ratio, x, r


def per_device(*arrays):
    def body(state):
        rounds, inverse, *_ = state
        again, ratio, x, r = one_round(inverse, *arrays)
        return jnp.where(again > 0, rounds - 1, 0), inverse * ratio, x, r

    field = arrays[0].shape[2:]
    start = (jnp.full((1,), ROUNDS, jnp.int32), jnp.ones((1,), F32), *call(zero_kernel, (field, field)))
    _, _, x, r = lax.while_loop(lambda state: state[0][0] > 0, body, start)
    return x[None, None], r[None, None]


def solution(mesh):
    return jax.shard_map(
        per_device,
        mesh=mesh,
        in_specs=(
            P("sec", "tile", None, None),
            P("sec", "tile", None, None),
            P("sec", "tile", None),
            P("sec", "tile", None),
            P("sec", "tile"),
            P("sec", "tile", None),
            P("sec", "tile", None),
            P("sec", "tile"),
            P("sec", "tile", None, None, None),
            P("sec", "tile", None, None, None),
        ),
        out_specs=(P("sec", "tile", None, None), P("sec", "tile", None, None)),
        check_vma=False,
    )
```

```python
import functools

import jax
import jax.numpy as jnp
from jax import lax
from jax.experimental import pallas as pl
from jax.experimental.pallas import tpu as pltpu
from jax.sharding import PartitionSpec as P

ITERS = 3
LARGE, ROUNDS = 1e37, 8
ROWS = 8
PASS_FLOPS = 20_000_000_000
F32, BF16 = jnp.float32, jnp.bfloat16
VMEM = pl.BlockSpec(memory_space=pltpu.VMEM)
CONTRACT_ROWS = (((0,), (0,)), ((), ()))
GROUP = 8


def split(x):
    high = x.astype(BF16)
    return jnp.concatenate([high, (x - high.astype(F32)).astype(BF16)], 1)


def fold(x):
    half = x.shape[1] // 2
    return x[:, :half] + x[:, half:]


def springs(hot, field, stiff_ref, scale, u_ref):
    slots, node = u_ref.shape
    diff = fold(lax.dot_general(hot, split(field), CONTRACT_ROWS, preferred_element_type=F32))
    rows = lax.broadcasted_iota(jnp.int32, (2 * GROUP, GROUP * node), 0) % GROUP
    cols = lax.broadcasted_iota(jnp.int32, (2 * GROUP, GROUP * node), 1) // node
    own = rows == cols
    for start in range(0, slots, GROUP):
        part = diff[start : start + GROUP]
        high = part.astype(BF16).astype(F32)
        both = jnp.concatenate([high, part - high], 0)
        wide = jnp.where(own, jnp.concatenate([both] * GROUP, 1), 0.0).astype(BF16)
        block = stiff_ref[0, 0, start : start + GROUP].reshape(GROUP * node, node)
        got = jnp.dot(wide, block, preferred_element_type=F32)
        u_ref[start : start + GROUP, :] = got[:GROUP] + got[GROUP:]
    u = u_ref[...] * scale
    spread = fold(jnp.dot(hot, split(u), preferred_element_type=F32))
    return spread, jnp.sum(diff * u, axis=0, keepdims=True)


def one_hot(near, far, count, blocks, paired=True):
    slots = near.shape[1]
    live = lax.broadcasted_iota(jnp.int32, (1, slots), 1) < count
    place = lax.broadcasted_iota(jnp.int32, (blocks, slots), 0)
    plus = jnp.where(live & (place == near), 1.0, 0.0)
    minus = jnp.where(live & paired & (place == far), 1.0, 0.0)
    return (plus - minus).astype(BF16)


def resident(ref):
    return lambda start: ref[0, 0, start : start + GROUP]


def fetched(ref, held, sems):
    pieces = sems.shape[0]
    chunk = held.shape[0] // pieces
    copies = []
    for piece in range(pieces):
        part = pl.ds(piece * chunk, chunk)
        copies.append(pltpu.make_async_copy(ref.at[0, 0, part], held.at[part], sems.at[piece]))
        copies[-1].start()

    def group(start):
        if start % chunk == 0:
            copies[start // chunk].wait()
        return held[start : start + GROUP]

    return group


def hot_kernel(section, tile, count, count_ex, *refs):
    own, far, near, prev = [r[...] for r in refs[:4]]
    hot_in, hot_ex = refs[5:]
    blk = hot_ex.shape[0] // 2
    far = far[0]
    there = tile[0] ^ (far // blk)
    place = ((there % 2) * 4 + there // 2) * blk + far % blk
    hot_in[...] = one_hot(own[0], place, count[0], 8 * blk)
    hot_ex[...] = one_hot(near[0], prev[0] + blk, count_ex[0], 2 * blk, section[0] > 0)


def zero_kernel(*outs):
    for out in outs:
        out[...] = jnp.zeros(out.shape, F32)


def pass_kernel(inverse, v_ref, out_ref, scale_ref):
    out_ref[...] = v_ref[...]
    scale_ref[...] = jnp.full(scale_ref.shape, inverse[0], F32)


def operator_kernel(step, n_fields, hot_in, hot_ex, scale_ref, in_ref, ex_ref, anchor_ref, row_ref, before_ref, *refs):
    fields = refs[:n_fields]
    mine_ref, other_ref, back_ref, row_out, u_in, u_ex, *held = refs[n_fields:]
    if held:
        copy = pltpu.make_async_copy(ex_ref, held[0], held[1])
        copy.start()
    blk = before_ref.shape[0]
    scale = scale_ref[...]
    field = jnp.concatenate([f[...] for f in fields], 0)
    spread, energy = springs(hot_in[...], field, in_ref, scale, u_in)
    v = field[:blk]
    if held:
        copy.wait()
        ex_ref = held[0]
    spread_ex, energy_ex = springs(hot_ex[...], jnp.concatenate([v, before_ref[...]], 0), ex_ref, scale, u_ex)
    back_ref[...] = spread_ex[blk:]
    image = anchor_ref[...] * v * scale
    energy = jnp.sum(image * v, axis=0, keepdims=True) + energy + energy_ex
    square = jnp.sum(v * v, axis=0, keepdims=True)
    rows = lax.broadcasted_iota(jnp.int32, row_ref.shape, 0)
    row = row_ref[...] + jnp.where(rows == 2 * step, square, 0.0) + jnp.where(rows == 2 * step + 1, energy, 0.0)
    row_out[...] = row
    mine = spread[: 4 * blk]
    other = spread[4 * blk :]
    tall = mine_ref.shape[0] // 4
    for j in range(4):
        block = mine[j * blk : (j + 1) * blk]
        if j == 0:
            block = block + image + spread_ex[:blk]
        mine_ref[j * tall : j * tall + blk, :] = block
        other_ref[j * tall : j * tall + blk, :] = other[j * blk : (j + 1) * blk]
        if tall > blk:
            mine_ref[j * tall + blk : (j + 1) * tall, :] = row
            other_ref[j * tall + blk : (j + 1) * tall, :] = row


def pair_kernel(mine_ref, got_ref, *outs):
    tall = mine_ref.shape[0] // 4
    for out, j in zip(outs, (0, 3, 1, 2)):
        out[...] = mine_ref[j * tall : (j + 1) * tall] + got_ref[j * tall : (j + 1) * tall]


def tree(values):
    while len(values) > 1:
        values = [a + b for a, b in zip(values[::2], values[1::2])]
    return values[0]


def sum_kernel(n, *refs):
    parts, incoming, out = refs[:n], refs[n], refs[n + 1]
    out[...] = tree([p[...] for p in parts]) + incoming[...]


def row_kernel(n, *refs):
    out = refs[n]
    rows = tree([p[p.shape[0] - out.shape[1] :] for p in refs[:n]])
    out[...] = jnp.broadcast_to(rows[None], out.shape)


def quadratic(coef, moments, shift):
    total = 0.0
    for i, a in enumerate(coef):
        for j, b in enumerate(coef):
            total = total + a * b * moments[i + j + shift]
    return total


def final_kernel(n, sums_ref, scale_ref, *refs):
    parts, incoming = refs[:n], refs[n]
    *vs, x_ref, r_ref, again_ref, ratio_ref = refs[n + 1 :]
    blk = incoming.shape[0]
    vs = [v[...] for v in vs] + [tree([p[:blk] for p in parts]) + incoming[...]]
    rows = jnp.sum(jnp.sum(sums_ref[...], axis=0), axis=1, keepdims=True)
    raw = [rows[j : j + 1] for j in range(2 * ITERS)]
    sigma = raw[1] / raw[0]
    inverse = 1.0 / sigma
    moments, scale = [], 1.0 / raw[0]
    for m in raw:
        moments.append(m * scale)
        scale = scale * inverse
    zero, one = jnp.zeros_like(sigma), jnp.ones_like(sigma)
    r, p, x = [one], [one], [zero]
    rr = one
    for step in range(ITERS):
        alpha = rr / quadratic(p, moments, 1)
        x = [a + alpha * b for a, b in zip(x + [zero] * (len(p) - len(x)), p)]
        q = [zero] + p
        r = [a - alpha * b for a, b in zip(r + [zero], q)]
        if step < ITERS - 1:
            new = quadratic(r, moments, 0)
            p = [a + (new / rr) * b for a, b in zip(r, p + [zero])]
            rr = new
    power = one
    x_sum, r_sum = 0.0, 0.0
    for k in range(ITERS + 1):
        v = vs[k]
        r_sum = r_sum + (r[k] * power) * v
        power = power * inverse
        if k < ITERS:
            x_sum = x_sum + (x[k] * power) * v
    x_ref[...] = x_sum * scale_ref[...]
    r_ref[...] = r_sum
    fine, ratio = jnp.abs(raw[1]) < LARGE, raw[0] / raw[1]
    for before, m in zip(raw[1:], raw[2:]):
        ratio = jnp.where(m < LARGE, before / m, ratio)
        fine = fine & (m < LARGE)
    again_ref[0] = jnp.max(jnp.where(fine, 0, 1))
    ratio_ref[0] = jnp.max(ratio)


def call(kernel, outs, *args, scratch=(), scalars=0, dtype=F32, flops=0, hbm=(), limit=16, scalar_outs=0):
    specs = [pl.BlockSpec(memory_space=pltpu.SMEM)] * scalars
    specs += [VMEM] * (len(args) - scalars)
    for i in hbm:
        specs[i] = pl.BlockSpec(memory_space=pltpu.HBM)
    dtypes = dtype if isinstance(dtype, tuple) else (dtype,) * len(outs)
    return pl.pallas_call(
        kernel,
        out_shape=[jax.ShapeDtypeStruct(o, d) for o, d in zip(outs, dtypes)],
        in_specs=specs,
        out_specs=[VMEM] * (len(outs) - scalar_outs) + [pl.BlockSpec(memory_space=pltpu.SMEM)] * scalar_outs,
        scratch_shapes=scratch,
        compiler_params=pltpu.CompilerParams(vmem_limit_bytes=limit * 2**20),
        cost_estimate=pl.CostEstimate(flops=flops, bytes_accessed=0, transcendentals=0) if flops else None,
    )(*args)


def swap(x, by):
    return lax.ppermute(x, "tile", [(i, i ^ by) for i in range(lax.axis_size("tile"))])


def shifted(x, by):
    peers = lax.axis_size("sec")
    return lax.ppermute(x, "sec", [(i, (i + by) % peers) for i in range(peers)])


def one_round(
    inverse,
    right_side,
    anchor_diag,
    intra_own,
    intra_far,
    intra_count,
    inter_own,
    inter_prev,
    inter_count,
    intra_stiff,
    inter_stiff,
):
    blk, node = right_side.shape[2:]
    anchor = anchor_diag[0, 0]
    section = lax.axis_index("sec").astype(jnp.int32).reshape(1)
    tile = lax.axis_index("tile").astype(jnp.int32).reshape(1)
    field, row = (blk, node), (ROWS, node)
    vs, moments = [right_side[0, 0]], jnp.zeros(row, F32)
    sections = lax.axis_size("sec")
    vs[0], scale = call(pass_kernel, (field, (1, node)), inverse, vs[0], scalars=1, flops=PASS_FLOPS)
    hot = call(
        hot_kernel, ((lax.axis_size("tile") * blk, intra_own.shape[2]), (2 * blk, inter_own.shape[2])),
        section, tile, intra_count.reshape(1), inter_count.reshape(1), intra_own, intra_far, inter_own, inter_prev, scale,
        scalars=4, dtype=BF16,
    )
    for step in range(ITERS):
        last = step == ITERS - 1
        tall = blk + ROWS if last else blk
        v = vs[-1]
        here = [v] + [swap(v, 2 * j) for j in (1, 2, 3)]
        fields = here + [swap(h, 1) for h in here]
        before = shifted(v, 1)
        scratch = [pltpu.VMEM((intra_own.shape[2], node), F32), pltpu.VMEM((inter_own.shape[2], node), F32)]
        if step == 0:
            scratch += [pltpu.VMEM(inter_stiff.shape, BF16), pltpu.SemaphoreType.DMA]
        mine, other, back, moments = call(
            functools.partial(operator_kernel, step, len(fields)), ((4 * tall, node), (4 * tall, node), field, row),
            *hot, scale, intra_stiff, inter_stiff, anchor, moments, before, *fields,
            scratch=scratch, hbm=(4,) if step == 0 else (),
        )
        incoming = shifted(back, -1)
        got = swap(other, 1)
        p0, p3, p1, p2 = call(pair_kernel, ((tall, node),) * 4, mine, got)
        parts = [p0] + [swap(p, 2 * j) for j, p in ((1, p1), (2, p2), (3, p3))]
        if not last:
            (nxt,) = call(functools.partial(sum_kernel, len(parts)), (field,), *parts, incoming)
            vs.append(nxt)
    (sums,) = call(functools.partial(row_kernel, len(parts)), ((sections, ROWS, node),), *parts)
    sums = lax.all_to_all(sums, "sec", 0, 0, tiled=True)
    x, r, again, ratio = call(
        functools.partial(final_kernel, len(parts)), (field, field, (1,), (1,)), sums, scale, *parts, incoming, *vs,
        dtype=(F32, F32, jnp.int32, F32), scalar_outs=2,
    )
    return again, ratio, x, r


def per_device(*arrays):
    def body(state):
        rounds, inverse, *_ = state
        again, ratio, x, r = one_round(inverse, *arrays)
        return jnp.where(again > 0, rounds - 1, 0), inverse * ratio, x, r

    field = arrays[0].shape[2:]
    start = (jnp.full((1,), ROUNDS, jnp.int32), jnp.ones((1,), F32), *call(zero_kernel, (field, field)))
    _, _, x, r = lax.while_loop(lambda state: state[0][0] > 0, body, start)
    return x[None, None], r[None, None]


def solution(mesh):
    return jax.shard_map(
        per_device,
        mesh=mesh,
        in_specs=(
            P("sec", "tile", None, None),
            P("sec", "tile", None, None),
            P("sec", "tile", None),
            P("sec", "tile", None),
            P("sec", "tile"),
            P("sec", "tile", None),
            P("sec", "tile", None),
            P("sec", "tile"),
            P("sec", "tile", None, None, None),
            P("sec", "tile", None, None, None),
        ),
        out_specs=(P("sec", "tile", None, None), P("sec", "tile", None, None)),
        check_vma=False,
    )
```

```python
import functools

import jax
import jax.numpy as jnp
from jax import lax
from jax.experimental import pallas as pl
from jax.experimental.pallas import tpu as pltpu
from jax.sharding import PartitionSpec as P

ITERS = 3
LARGE, ROUNDS = 1e37, 8
ROWS = 8
PASS_FLOPS = 20_000_000_000
F32, BF16 = jnp.float32, jnp.bfloat16
VMEM = pl.BlockSpec(memory_space=pltpu.VMEM)
CONTRACT_ROWS = (((0,), (0,)), ((), ()))
GROUP = 8


def split(x):
    high = x.astype(BF16)
    return jnp.concatenate([high, (x - high.astype(F32)).astype(BF16)], 1)


def fold(x):
    half = x.shape[1] // 2
    return x[:, :half] + x[:, half:]


def springs(hot, field, stiff_ref, scale, u_ref):
    slots, node = u_ref.shape
    diff = fold(lax.dot_general(hot, split(field), CONTRACT_ROWS, preferred_element_type=F32))
    rows = lax.broadcasted_iota(jnp.int32, (2 * GROUP, GROUP * node), 0) % GROUP
    cols = lax.broadcasted_iota(jnp.int32, (2 * GROUP, GROUP * node), 1) // node
    own = rows == cols
    for start in range(0, slots, GROUP):
        part = diff[start : start + GROUP]
        high = part.astype(BF16).astype(F32)
        both = jnp.concatenate([high, part - high], 0)
        wide = jnp.where(own, jnp.concatenate([both] * GROUP, 1), 0.0).astype(BF16)
        block = stiff_ref[0, 0, start : start + GROUP].reshape(GROUP * node, node)
        got = jnp.dot(wide, block, preferred_element_type=F32)
        u_ref[start : start + GROUP, :] = got[:GROUP] + got[GROUP:]
    u = u_ref[...] * scale
    spread = fold(jnp.dot(hot, split(u), preferred_element_type=F32))
    return spread, jnp.sum(diff * u, axis=0, keepdims=True)


def one_hot(near, far, count, blocks, paired=True):
    slots = near.shape[1]
    live = lax.broadcasted_iota(jnp.int32, (1, slots), 1) < count
    place = lax.broadcasted_iota(jnp.int32, (blocks, slots), 0)
    plus = jnp.where(live & (place == near), 1.0, 0.0)
    minus = jnp.where(live & paired & (place == far), 1.0, 0.0)
    return (plus - minus).astype(BF16)


def resident(ref):
    return lambda start: ref[0, 0, start : start + GROUP]


def fetched(ref, held, sems):
    pieces = sems.shape[0]
    chunk = held.shape[0] // pieces
    copies = []
    for piece in range(pieces):
        part = pl.ds(piece * chunk, chunk)
        copies.append(pltpu.make_async_copy(ref.at[0, 0, part], held.at[part], sems.at[piece]))
        copies[-1].start()

    def group(start):
        if start % chunk == 0:
            copies[start // chunk].wait()
        return held[start : start + GROUP]

    return group


def hot_kernel(section, tile, count, count_ex, *refs):
    own, far, near, prev = [r[...] for r in refs[:4]]
    hot_in, hot_ex = refs[5:]
    blk = hot_ex.shape[0] // 2
    far = far[0]
    there = tile[0] ^ (far // blk)
    place = ((there % 2) * 4 + there // 2) * blk + far % blk
    hot_in[...] = one_hot(own[0], place, count[0], 8 * blk)
    hot_ex[...] = one_hot(near[0], prev[0] + blk, count_ex[0], 2 * blk, section[0] > 0)


def zero_kernel(*outs):
    for out in outs:
        out[...] = jnp.zeros(out.shape, F32)


def pass_kernel(inverse, v_ref, out_ref, scale_ref):
    out_ref[...] = v_ref[...]
    scale_ref[...] = jnp.full(scale_ref.shape, inverse[0], F32)


def operator_kernel(step, n_fields, hot_in, hot_ex, scale_ref, in_ref, ex_ref, anchor_ref, row_ref, before_ref, *refs):
    fields = refs[:n_fields]
    mine_ref, other_ref, back_ref, row_out, u_in, u_ex = refs[n_fields:]
    blk = before_ref.shape[0]
    scale = scale_ref[...]
    field = jnp.concatenate([f[...] for f in fields], 0)
    spread, energy = springs(hot_in[...], field, in_ref, scale, u_in)
    v = field[:blk]
    spread_ex, energy_ex = springs(hot_ex[...], jnp.concatenate([v, before_ref[...]], 0), ex_ref, scale, u_ex)
    back_ref[...] = spread_ex[blk:]
    image = anchor_ref[...] * v * scale
    energy = jnp.sum(image * v, axis=0, keepdims=True) + energy + energy_ex
    square = jnp.sum(v * v, axis=0, keepdims=True)
    rows = lax.broadcasted_iota(jnp.int32, row_ref.shape, 0)
    row = row_ref[...] + jnp.where(rows == 2 * step, square, 0.0) + jnp.where(rows == 2 * step + 1, energy, 0.0)
    row_out[...] = row
    mine = spread[: 4 * blk]
    other = spread[4 * blk :]
    tall = mine_ref.shape[0] // 4
    for j in range(4):
        block = mine[j * blk : (j + 1) * blk]
        if j == 0:
            block = block + image + spread_ex[:blk]
        mine_ref[j * tall : j * tall + blk, :] = block
        other_ref[j * tall : j * tall + blk, :] = other[j * blk : (j + 1) * blk]
        if tall > blk:
            mine_ref[j * tall + blk : (j + 1) * tall, :] = row
            other_ref[j * tall + blk : (j + 1) * tall, :] = row


def pair_kernel(mine_ref, got_ref, *outs):
    tall = mine_ref.shape[0] // 4
    for out, j in zip(outs, (0, 3, 1, 2)):
        out[...] = mine_ref[j * tall : (j + 1) * tall] + got_ref[j * tall : (j + 1) * tall]


def tree(values):
    while len(values) > 1:
        values = [a + b for a, b in zip(values[::2], values[1::2])]
    return values[0]


def sum_kernel(n, *refs):
    parts, incoming, out = refs[:n], refs[n], refs[n + 1]
    out[...] = tree([p[...] for p in parts]) + incoming[...]


def row_kernel(n, *refs):
    out = refs[n]
    rows = tree([p[p.shape[0] - out.shape[1] :] for p in refs[:n]])
    out[...] = jnp.broadcast_to(rows[None], out.shape)


def quadratic(coef, moments, shift):
    total = 0.0
    for i, a in enumerate(coef):
        for j, b in enumerate(coef):
            total = total + a * b * moments[i + j + shift]
    return total


def final_kernel(n, sums_ref, scale_ref, *refs):
    parts, incoming = refs[:n], refs[n]
    *vs, x_ref, r_ref, again_ref, ratio_ref = refs[n + 1 :]
    blk = incoming.shape[0]
    vs = [v[...] for v in vs] + [tree([p[:blk] for p in parts]) + incoming[...]]
    rows = jnp.sum(jnp.sum(sums_ref[...], axis=0), axis=1, keepdims=True)
    raw = [rows[j : j + 1] for j in range(2 * ITERS)]
    sigma = raw[1] / raw[0]
    inverse = 1.0 / sigma
    moments, scale = [], 1.0 / raw[0]
    for m in raw:
        moments.append(m * scale)
        scale = scale * inverse
    zero, one = jnp.zeros_like(sigma), jnp.ones_like(sigma)
    r, p, x = [one], [one], [zero]
    rr = one
    for step in range(ITERS):
        alpha = rr / quadratic(p, moments, 1)
        x = [a + alpha * b for a, b in zip(x + [zero] * (len(p) - len(x)), p)]
        q = [zero] + p
        r = [a - alpha * b for a, b in zip(r + [zero], q)]
        if step < ITERS - 1:
            new = quadratic(r, moments, 0)
            p = [a + (new / rr) * b for a, b in zip(r, p + [zero])]
            rr = new
    power = one
    x_sum, r_sum = 0.0, 0.0
    for k in range(ITERS + 1):
        v = vs[k]
        r_sum = r_sum + (r[k] * power) * v
        power = power * inverse
        if k < ITERS:
            x_sum = x_sum + (x[k] * power) * v
    x_ref[...] = x_sum * scale_ref[...]
    r_ref[...] = r_sum
    fine, ratio = jnp.abs(raw[1]) < LARGE, raw[0] / raw[1]
    for before, m in zip(raw[1:], raw[2:]):
        ratio = jnp.where(m < LARGE, before / m, ratio)
        fine = fine & (m < LARGE)
    again_ref[0] = jnp.max(jnp.where(fine, 0, 1))
    ratio_ref[0] = jnp.max(ratio)


def call(kernel, outs, *args, scratch=(), scalars=0, dtype=F32, flops=0, hbm=False, limit=16, scalar_outs=0):
    specs = [pl.BlockSpec(memory_space=pltpu.SMEM)] * scalars
    specs += [pl.BlockSpec(memory_space=pltpu.HBM) if hbm else VMEM] * (len(args) - scalars)
    dtypes = dtype if isinstance(dtype, tuple) else (dtype,) * len(outs)
    return pl.pallas_call(
        kernel,
        out_shape=[jax.ShapeDtypeStruct(o, d) for o, d in zip(outs, dtypes)],
        in_specs=specs,
        out_specs=[VMEM] * (len(outs) - scalar_outs) + [pl.BlockSpec(memory_space=pltpu.SMEM)] * scalar_outs,
        scratch_shapes=scratch,
        compiler_params=pltpu.CompilerParams(vmem_limit_bytes=limit * 2**20),
        cost_estimate=pl.CostEstimate(flops=flops, bytes_accessed=0, transcendentals=0) if flops else None,
    )(*args)


def swap(x, by):
    return lax.ppermute(x, "tile", [(i, i ^ by) for i in range(lax.axis_size("tile"))])


def shifted(x, by, wrap=True):
    peers = lax.axis_size("sec")
    return lax.ppermute(x, "sec", [(i, (i + by) % peers) for i in range(peers) if wrap or 0 <= i + by < peers])


def one_round(
    inverse,
    right_side,
    anchor_diag,
    intra_own,
    intra_far,
    intra_count,
    inter_own,
    inter_prev,
    inter_count,
    intra_stiff,
    inter_stiff,
):
    blk, node = right_side.shape[2:]
    anchor = anchor_diag[0, 0]
    section = lax.axis_index("sec").astype(jnp.int32).reshape(1)
    tile = lax.axis_index("tile").astype(jnp.int32).reshape(1)
    field, row = (blk, node), (ROWS, node)
    vs, moments = [right_side[0, 0]], jnp.zeros(row, F32)
    sections = lax.axis_size("sec")
    vs[0], scale = call(pass_kernel, (field, (1, node)), inverse, vs[0], scalars=1, flops=PASS_FLOPS)
    hot = call(
        hot_kernel, ((lax.axis_size("tile") * blk, intra_own.shape[2]), (2 * blk, inter_own.shape[2])),
        section, tile, intra_count.reshape(1), inter_count.reshape(1), intra_own, intra_far, inter_own, inter_prev, scale,
        scalars=4, dtype=BF16,
    )
    for step in range(ITERS):
        last = step == ITERS - 1
        tall = blk + ROWS if last else blk
        v = vs[-1]
        here = [v] + [swap(v, 2 * j) for j in (1, 2, 3)]
        fields = here + [swap(h, 1) for h in here]
        before = shifted(v, 1)
        mine, other, back, moments = call(
            functools.partial(operator_kernel, step, len(fields)), ((4 * tall, node), (4 * tall, node), field, row),
            *hot, scale, intra_stiff, inter_stiff, anchor, moments, before, *fields,
            scratch=[pltpu.VMEM((intra_own.shape[2], node), F32), pltpu.VMEM((inter_own.shape[2], node), F32)],
        )
        incoming = shifted(back, -1, not last)
        got = swap(other, 1)
        p0, p3, p1, p2 = call(pair_kernel, ((tall, node),) * 4, mine, got)
        parts = [p0] + [swap(p, 2 * j) for j, p in ((1, p1), (2, p2), (3, p3))]
        if not last:
            (nxt,) = call(functools.partial(sum_kernel, len(parts)), (field,), *parts, incoming)
            vs.append(nxt)
    (sums,) = call(functools.partial(row_kernel, len(parts)), ((sections, ROWS, node),), *parts)
    sums = lax.all_to_all(sums, "sec", 0, 0, tiled=True)
    x, r, again, ratio = call(
        functools.partial(final_kernel, len(parts)), (field, field, (1,), (1,)), sums, scale, *parts, incoming, *vs,
        dtype=(F32, F32, jnp.int32, F32), scalar_outs=2,
    )
    return again, ratio, x, r


def per_device(*arrays):
    def body(state):
        rounds, inverse, *_ = state
        again, ratio, x, r = one_round(inverse, *arrays)
        return jnp.where(again > 0, rounds - 1, 0), inverse * ratio, x, r

    field = arrays[0].shape[2:]
    start = (jnp.full((1,), ROUNDS, jnp.int32), jnp.ones((1,), F32), *call(zero_kernel, (field, field)))
    _, _, x, r = lax.while_loop(lambda state: state[0][0] > 0, body, start)
    return x[None, None], r[None, None]


def solution(mesh):
    return jax.shard_map(
        per_device,
        mesh=mesh,
        in_specs=(
            P("sec", "tile", None, None),
            P("sec", "tile", None, None),
            P("sec", "tile", None),
            P("sec", "tile", None),
            P("sec", "tile"),
            P("sec", "tile", None),
            P("sec", "tile", None),
            P("sec", "tile"),
            P("sec", "tile", None, None, None),
            P("sec", "tile", None, None, None),
        ),
        out_specs=(P("sec", "tile", None, None), P("sec", "tile", None, None)),
        check_vma=False,
    )
```
